32 devices in a mesh: expert: 16 (over z, x, core), dp: 2 (over y).
Axes of the slice: x: 2, y: 2, z: 4, core: 2. Of those that a mesh axis runs over, the one named last changes fastest.
Arguments:
- tokens: bfloat16 [64, 2048], P('dp'), may hold values from -6 to 6
- w_gate: bfloat16 [32, 768, 2048], P('expert', 'dp'), may hold values from -2 to 2
- w_up: bfloat16 [32, 768, 2048], P('expert', 'dp'), may hold values from -2 to 2
- w_down: bfloat16 [32, 768, 2048], P('expert', 'dp'), may hold values from -2 to 2
Outputs:
- cosine: float32 [64, 32, 32], P('expert')
The draws below stay inside these ranges and needn't reach their ends.
All inputs are finite; a program needn't handle non-finite values.
Results may differ from the reference program's by a relative error of at most 0.0014.
Values may be sent and summed in bfloat16 or wider, within the bound.
A program may use at most 64 MiB of HBM per device.

```python
import jax
import jax.numpy as jnp
from jax import lax

D = 2048
H = 768
E = 32
TOKENS = 64


def expert_mix(key):
    return jax.random.uniform(jax.random.fold_in(key, 7), (E,), jnp.float32, 0.0, 0.95)


def mixed_weight(key, salt, shape, fan_in):
    common_key = jax.random.fold_in(key, salt)
    own_key = jax.random.fold_in(key, salt + 100)
    common = jax.random.normal(common_key, shape[1:], jnp.float32)
    own = jax.random.normal(own_key, shape, jnp.float32)
    mixing = expert_mix(key)[:, None, None]
    return (mixing * common[None] + jnp.sqrt(1.0 - mixing * mixing) * own) * fan_in ** (-0.5)


def draw_w_gate(key, part):
    return jnp.clip(mixed_weight(key, 11, (E, H, D), D), -2.0, 2.0).astype(jnp.bfloat16)


def draw_w_up(key, part):
    return jnp.clip(mixed_weight(key, 12, (E, H, D), D), -2.0, 2.0).astype(jnp.bfloat16)


def draw_w_down(key, part):
    column_scale = jnp.exp(jax.random.uniform(jax.random.fold_in(key, 313), (D,), jnp.float32, -1.15, 1.15))
    scaled = mixed_weight(key, 13, (E, H, D), H) * column_scale[None, None, :]
    return jnp.clip(scaled, -2.0, 2.0).astype(jnp.bfloat16)


def block_scale(stream_key, dims, cuts, low, high):
    def one(axis_at, blocks):
        heights = jax.random.uniform(jax.random.fold_in(jax.random.fold_in(stream_key, 6), axis_at), (blocks,), jnp.float32, low / len(cuts), high / len(cuts))
        return jnp.repeat(jnp.exp(heights), dims[axis_at] // blocks).reshape((-1,) + (1,) * (len(dims) - axis_at - 1))

    loudness = one(*cuts[0])
    for cut in cuts[1:]:
        loudness = loudness * one(*cut)
    return loudness


def bell_draw(key, extent, deviation, bound, cuts=(), held_as=jnp.bfloat16):
    factor_of = block_scale(key, extent, cuts, -0.22, 0.18) if cuts else 1.0
    array = jax.random.normal(key, extent, jnp.float32) * deviation * factor_of
    return jnp.minimum(jnp.maximum(array, -bound), bound).astype(held_as)


def setup_inputs(seed: int = 0) -> dict:
    streams_of = jax.random.split(jax.random.key(seed), 5)
    return {
        "tokens": bell_draw(streams_of[0], (TOKENS, D), 1.0, 6.0, ((0, 2),)),
        "w_gate": draw_w_gate(jax.random.fold_in(streams_of[4], 71), 0),
        "w_up": draw_w_up(jax.random.fold_in(streams_of[4], 71), 0),
        "w_down": draw_w_down(jax.random.fold_in(streams_of[4], 71), 0),
    }


def expert_outputs(tokens, gate_row, up_row, down_row):
    gate = jnp.dot(tokens, gate_row.T, preferred_element_type=jnp.float32)
    upward = jnp.dot(tokens, up_row.T, preferred_element_type=jnp.float32)
    hidden = (jax.nn.silu(gate) * upward).astype(jnp.bfloat16)
    total = jnp.dot(hidden, down_row, preferred_element_type=jnp.float32)
    return total.astype(jnp.bfloat16)

def reference(tokens, w_gate, w_up, w_down):
    outputs = lax.map(lambda weights: expert_outputs(tokens, weights[0], weights[1], weights[2]), (w_gate, w_up, w_down))
    wide = outputs.astype(jnp.float32)
    gram = jnp.einsum('etf,gtf->teg', wide, wide)
    diagonal = jnp.diagonal(gram, axis1=1, axis2=2)
    inverse = lax.rsqrt(diagonal + 1e-06)
    return gram * inverse[:, :, None] * inverse[:, None, :]
```

```python
import functools

import jax
import jax.numpy as jnp
from jax import lax
from jax.experimental import pallas as pl
from jax.experimental.pallas import tpu as pltpu
from jax.sharding import PartitionSpec as P

F32 = jnp.float32
BF16 = jnp.bfloat16
MESH = pl.DeviceIdType.MESH


def log2(n):
    assert n & (n - 1) == 0
    return n.bit_length() - 1


def matrix_of(rows, cols, want, keep=None):
    r = lax.broadcasted_iota(jnp.int32, (rows, cols), 0)
    q = lax.broadcasted_iota(jnp.int32, (rows, cols), 1)
    hit = q == want(r)
    if keep is not None:
        hit = hit & keep(r)
    return jnp.where(hit, 1.0, 0.0).astype(BF16)


def kernel(cfg, tok_hbm, wg_hbm, wu_hbm, wd_hbm, out_ref,
           tok, wg, wu, wd, perm_send, perm_recv, own, ysend, yrecv, xsend, xrecv,
           gsend, grecv,
           w_sem, t_sem, ts_sem, tr_sem, ys_sem, yr_sem, xs_sem, xr_sem, gs_sem, gr_sem):
    n_dp, n_ex, T, Tl, D, H, E_loc, ec, G, L, Tk = cfg
    E = n_ex * E_loc
    Fk = D // n_dp
    R = ec * G * Tk
    chunks = E_loc // ec
    dp = lax.axis_index("dp")
    ex = lax.axis_index("expert")

    def dp_peer(s):
        return lax.rem(dp + s, n_dp)

    own_tok = pltpu.make_async_copy(tok_hbm, tok.at[dp], t_sem)
    own_tok.start()
    loads = {}
    for e in range(E_loc):
        for k, (src, dst) in enumerate(((wg_hbm, wg), (wu_hbm, wu), (wd_hbm, wd))):
            loads[e, k] = pltpu.make_async_copy(src.at[e], dst.at[e], w_sem.at[e, k])
            loads[e, k].start()

    barrier = pltpu.get_barrier_semaphore()
    for s in range(1, n_dp):
        pl.semaphore_signal(barrier, inc=1, device_id=(ex, dp_peer(s)), device_id_type=MESH)

    def greet(s, carry):
        pl.semaphore_signal(
            barrier, inc=1, device_id=(lax.rem(ex + s, n_ex), dp), device_id_type=MESH
        )
        return carry

    lax.fori_loop(1, n_ex, greet, 0)
    pl.semaphore_wait(barrier, n_dp - 1 + n_ex - 1)

    tok_copies = []
    for s in range(1, n_dp):
        copy = pltpu.make_async_remote_copy(
            src_ref=tok_hbm, dst_ref=tok.at[dp],
            send_sem=ts_sem.at[s - 1], recv_sem=tr_sem.at[s - 1],
            device_id=(ex, dp_peer(s)), device_id_type=MESH,
        )
        copy.start()
        tok_copies.append(copy)

    GE = ec * G
    rows = GE * T
    lR, lTk = log2(R), log2(Tk)
    perm_send[...] = matrix_of(
        rows, rows,
        lambda r: ((r >> lTk) & (GE - 1)) * T + (r >> lR) * Tk + (r & (Tk - 1)),
    )
    lE, lEl, lec = log2(E), log2(E_loc), log2(ec)

    for c in range(chunks):
        def want(r):
            g = r >> (lTk + lE)
            j = (r >> lE) & (Tk - 1)
            e = r & (E - 1)
            el = e & (ec - 1)
            return (e >> lEl) * R + (el * G + g) * Tk + j

        perm_recv[c] = matrix_of(
            G * Tk * E, n_ex * R, want,
            lambda r: ((r & (E_loc - 1)) >> lec) == c,
        )

    own_tok.wait()
    for copy in tok_copies:
        copy.wait_recv()
    tokens = tok[...].reshape(T, D)

    nt = (((1,), (1,)), ((), ()))
    y_copies = {}
    for e in range(E_loc):
        loads[e, 0].wait()
        gate = lax.dot_general(tokens, wg[e], nt, preferred_element_type=F32)
        loads[e, 1].wait()
        up = lax.dot_general(tokens, wu[e], nt, preferred_element_type=F32)
        hidden = (gate / (1.0 + jnp.exp(-gate)) * up).astype(BF16)
        loads[e, 2].wait()
        for s in range(1, n_dp):
            cols = pl.ds(pl.multiple_of(dp_peer(s) * Fk, Fk), Fk)
            part = jnp.dot(hidden, wd[e, :, cols], preferred_element_type=F32)
            ysend[e, s - 1] = part.astype(BF16)
            copy = pltpu.make_async_remote_copy(
                src_ref=ysend.at[e, s - 1], dst_ref=yrecv.at[e, s - 1],
                send_sem=ys_sem.at[e, s - 1], recv_sem=yr_sem.at[e, s - 1],
                device_id=(ex, dp_peer(s)), device_id_type=MESH,
            )
            copy.start()
            y_copies[e, s] = copy
        cols = pl.ds(pl.multiple_of(dp * Fk, Fk), Fk)
        own[e] = jnp.dot(hidden, wd[e, :, cols], preferred_element_type=F32)

    for c in range(chunks):
        pieces = []
        for e in range(c * ec, (c + 1) * ec):
            total = own[e]
            for s in range(1, n_dp):
                y_copies[e, s].wait_recv()
                total += yrecv[e, s - 1].astype(F32)
            total = total.astype(BF16)
            pieces += [total[:, g * L:(g + 1) * L] for g in range(G)]
        stacked = jnp.concatenate(pieces, axis=0)
        xsend[c] = jnp.dot(
            perm_send[...], stacked, preferred_element_type=F32
        ).astype(BF16)
        mine = pl.ds(pl.multiple_of(ex * R, R), R)

        def send(s, carry):
            to = lax.rem(ex + s, n_ex)
            theirs = pl.ds(pl.multiple_of(to * R, R), R)
            pltpu.make_async_remote_copy(
                src_ref=xsend.at[c, theirs], dst_ref=xrecv.at[c, mine],
                send_sem=xs_sem.at[c], recv_sem=xr_sem.at[c],
                device_id=(to, dp), device_id_type=MESH,
            ).start()
            return carry

        lax.fori_loop(1, n_ex, send, 0, unroll=n_ex <= 16)
        xrecv[c, mine] = xsend[c, mine]

    total = None
    for c in range(chunks):
        most = xrecv.at[c, pl.ds(0, (n_ex - 1) * R)]
        pltpu.make_async_copy(most, most, xr_sem.at[c]).wait()
        term = jnp.dot(perm_recv[c], xrecv[c], preferred_element_type=F32)
        total = term if total is None else total + term
    total = total.astype(BF16)
    per_token = jnp.concatenate(
        [total[g * Tk * E:(g + 1) * Tk * E] for g in range(G)], axis=1
    )
    full = lax.dot_general(per_token, per_token, nt, preferred_element_type=F32)
    lane = lax.broadcasted_iota(jnp.int32, (E, Tk * E), 1)
    row = lax.broadcasted_iota(jnp.int32, (E, Tk * E), 0)
    gram = jnp.zeros((E, Tk * E), F32)
    for j in range(Tk):
        gram = jnp.where((lane >> lE) == j, full[j * E:(j + 1) * E], gram)
    gsend[...] = gram
    g_copies = []
    for s in range(1, n_dp):
        copy = pltpu.make_async_remote_copy(
            src_ref=gsend, dst_ref=grecv.at[s - 1],
            send_sem=gs_sem.at[s - 1], recv_sem=gr_sem.at[s - 1],
            device_id=(ex, dp_peer(s)), device_id_type=MESH,
        )
        copy.start()
        g_copies.append(copy)
    for copy in tok_copies:
        copy.wait_send()
    for copy in y_copies.values():
        copy.wait_send()
    for c in range(chunks):
        most = xsend.at[c, pl.ds(0, (n_ex - 1) * R)]
        pltpu.make_async_copy(most, most, xs_sem.at[c]).wait()
    for s in range(1, n_dp):
        g_copies[s - 1].wait_recv()
        gram += grecv[s - 1]
    diagonal = jnp.where((lane & (E - 1)) == row, gram, 0.0)
    along = lax.rsqrt(jnp.sum(diagonal, axis=0, keepdims=True) + 1e-06)
    for j in range(Tk):
        block = slice(j * E, (j + 1) * E)
        down = lax.rsqrt(jnp.sum(diagonal[:, block], axis=1, keepdims=True) + 1e-06)
        out_ref[j] = gram[:, block] * down * along[:, block]
    for copy in g_copies:
        copy.wait_send()


def shards(n_dp, n_ex, tokens, w_gate, w_up, w_down):
    Tl, D = tokens.shape
    E_loc, H, _ = w_gate.shape
    T = Tl * n_dp
    Tk = T // n_ex
    Fk = D // n_dp
    ec = 1 if Tk * (Fk // 128) >= 16 else E_loc
    G = max(1, 16 // (Tk * ec))
    L = Fk // G
    R = ec * G * Tk
    E = n_ex * E_loc
    chunks = E_loc // ec
    cfg = (n_dp, n_ex, T, Tl, D, H, E_loc, ec, G, L, Tk)
    dma = pltpu.SemaphoreType.DMA
    peers = n_dp - 1
    return pl.pallas_call(
        functools.partial(kernel, cfg),
        out_shape=jax.ShapeDtypeStruct((Tk, E, E), F32),
        in_specs=[pl.BlockSpec(memory_space=pl.ANY)] * 4,
        out_specs=pl.BlockSpec(memory_space=pltpu.VMEM),
        scratch_shapes=[
            pltpu.VMEM((n_dp, Tl, D), BF16),
            pltpu.VMEM((E_loc, H, D), BF16),
            pltpu.VMEM((E_loc, H, D), BF16),
            pltpu.VMEM((E_loc, H, D), BF16),
            pltpu.VMEM((ec * G * T, ec * G * T), BF16),
            pltpu.VMEM((chunks, G * Tk * E, n_ex * R), BF16),
            pltpu.VMEM((E_loc, T, Fk), F32),
            pltpu.VMEM((E_loc, peers, T, Fk), BF16),
            pltpu.VMEM((E_loc, peers, T, Fk), BF16),
            pltpu.VMEM((chunks, n_ex * R, L), BF16),
            pltpu.VMEM((chunks, n_ex * R, L), BF16),
            pltpu.VMEM((E, Tk * E), F32),
            pltpu.VMEM((peers, E, Tk * E), F32),
            dma((E_loc, 3)),
            dma,
            dma((peers,)),
            dma((peers,)),
            dma((E_loc, peers)),
            dma((E_loc, peers)),
            dma((chunks,)),
            dma((chunks,)),
            dma((peers,)),
            dma((peers,)),
        ],
        compiler_params=pltpu.CompilerParams(
            collective_id=0, has_side_effects=True, vmem_limit_bytes=48 * 1024 * 1024
        ),
        cost_estimate=pl.CostEstimate(
            flops=6 * E_loc * T * D * H, bytes_accessed=6 * E_loc * H * D,
            transcendentals=E_loc * T * H,
        ),
    )(tokens, w_gate, w_up, w_down)


def solution(mesh):
    placed = (
        P("dp", None),
        P("expert", "dp", None),
        P("expert", "dp", None),
        P("expert", "dp", None),
    )
    return jax.shard_map(
        functools.partial(shards, mesh.shape["dp"], mesh.shape["expert"]),
        mesh=mesh, in_specs=placed, out_specs=P("expert", None, None), check_vma=False,
    )
```

```python
import functools

import jax
import jax.numpy as jnp
from jax import lax
from jax.experimental import pallas as pl
from jax.experimental.pallas import tpu as pltpu
from jax.sharding import PartitionSpec as P

F32 = jnp.float32
BF16 = jnp.bfloat16
MESH = pl.DeviceIdType.MESH


def log2(n):
    assert n & (n - 1) == 0
    return n.bit_length() - 1


def matrix_of(rows, cols, want, keep=None):
    r = lax.broadcasted_iota(jnp.int32, (rows, cols), 0)
    q = lax.broadcasted_iota(jnp.int32, (rows, cols), 1)
    hit = q == want(r)
    if keep is not None:
        hit = hit & keep(r)
    return jnp.where(hit, 1.0, 0.0).astype(BF16)


def kernel(cfg, tok_hbm, wg_hbm, wu_hbm, wd_hbm, out_ref,
           tok, wg, wu, wd, perm_send, perm_recv, own, ysend, yrecv, xsend, xrecv,
           gsend, grecv,
           w_sem, t_sem, ts_sem, tr_sem, ys_sem, yr_sem, xs_sem, xr_sem, gs_sem, gr_sem):
    n_dp, n_ex, T, Tl, D, H, E_loc, ec, G, L, Tk = cfg
    E = n_ex * E_loc
    Fk = D // n_dp
    R = ec * G * Tk
    chunks = E_loc // ec
    dp = lax.axis_index("dp")
    ex = lax.axis_index("expert")

    def dp_peer(s):
        return lax.rem(dp + s, n_dp)

    barrier = pltpu.get_barrier_semaphore()
    for s in range(1, n_dp):
        pl.semaphore_signal(barrier, inc=1, device_id=(ex, dp_peer(s)), device_id_type=MESH)

    def greet(s, carry):
        pl.semaphore_signal(
            barrier, inc=1, device_id=(lax.rem(ex + s, n_ex), dp), device_id_type=MESH
        )
        return carry

    lax.fori_loop(1, n_ex, greet, 0)

    own_tok = pltpu.make_async_copy(tok_hbm, tok.at[0], t_sem)
    own_tok.start()
    loads = {}
    for e in range(E_loc):
        for k, (src, dst) in enumerate(((wg_hbm, wg), (wu_hbm, wu), (wd_hbm, wd))):
            loads[e, k] = pltpu.make_async_copy(src.at[e], dst.at[e], w_sem.at[e, k])
            loads[e, k].start()

    pl.semaphore_wait(barrier, n_dp - 1 + n_ex - 1)

    tok_copies = []
    for s in range(1, n_dp):
        copy = pltpu.make_async_remote_copy(
            src_ref=tok_hbm, dst_ref=tok.at[s],
            send_sem=ts_sem.at[s - 1], recv_sem=tr_sem.at[s - 1],
            device_id=(ex, dp_peer(s)), device_id_type=MESH,
        )
        copy.start()
        tok_copies.append(copy)

    nt = (((1,), (1,)), ((), ()))
    y_copies = {}

    def hidden_of(tokens, e):
        gate = lax.dot_general(tokens, wg[e], nt, preferred_element_type=F32)
        up = lax.dot_general(tokens, wu[e], nt, preferred_element_type=F32)
        return (gate / (1.0 + jnp.exp(-gate)) * up).astype(BF16)

    def project_theirs(hidden, e, slots):
        for s in range(1, n_dp):
            cols = pl.ds(pl.multiple_of(dp_peer(s) * Fk, Fk), Fk)
            part = jnp.dot(hidden, wd[e, :, cols], preferred_element_type=F32).astype(BF16)
            for n, k in enumerate(slots):
                owner = lax.rem(dp + n_dp - k, n_dp)
                ysend[e, s - 1, owner] = part[n * Tl:(n + 1) * Tl]
                copy = pltpu.make_async_remote_copy(
                    src_ref=ysend.at[e, s - 1, owner], dst_ref=yrecv.at[e, s - 1, owner],
                    send_sem=ys_sem.at[e, s - 1, k], recv_sem=yr_sem.at[e, s - 1, k],
                    device_id=(ex, dp_peer(s)), device_id_type=MESH,
                )
                copy.start()
                y_copies[e, s, k] = copy

    def project_mine(hidden, e, slots):
        cols = pl.ds(pl.multiple_of(dp * Fk, Fk), Fk)
        part = jnp.dot(hidden, wd[e, :, cols], preferred_element_type=F32)
        for n, k in enumerate(slots):
            own[e, lax.rem(dp + n_dp - k, n_dp)] = part[n * Tl:(n + 1) * Tl]

    own_tok.wait()
    for e in range(E_loc):
        loads[e, 0].wait()
        loads[e, 1].wait()
        hidden = hidden_of(tok[0], e)
        loads[e, 2].wait()
        project_theirs(hidden, e, (0,))
        project_mine(hidden, e, (0,))

    GE = ec * G
    rows = GE * T
    lR, lTk = log2(R), log2(Tk)
    perm_send[...] = matrix_of(
        rows, rows,
        lambda r: ((r >> lTk) & (GE - 1)) * T + (r >> lR) * Tk + (r & (Tk - 1)),
    )
    lE, lEl, lec = log2(E), log2(E_loc), log2(ec)

    for c in range(chunks):
        def want(r):
            g = r >> (lTk + lE)
            j = (r >> lE) & (Tk - 1)
            e = r & (E - 1)
            el = e & (ec - 1)
            return (e >> lEl) * R + (el * G + g) * Tk + j

        perm_recv[c] = matrix_of(
            G * Tk * E, n_ex * R, want,
            lambda r: ((r & (E_loc - 1)) >> lec) == c,
        )

    for copy in tok_copies:
        copy.wait_recv()
    if n_dp > 1:
        hidden = []
        for e in range(E_loc):
            hidden.append(hidden_of(tok[1:].reshape(T - Tl, D), e))
            project_theirs(hidden[e], e, range(1, n_dp))
        for e in range(E_loc):
            project_mine(hidden[e], e, range(1, n_dp))

    for c in range(chunks):
        pieces = []
        for e in range(c * ec, (c + 1) * ec):
            total = own[e].reshape(T, Fk)
            for s in range(1, n_dp):
                for k in range(n_dp):
                    y_copies[e, s, k].wait_recv()
                total += yrecv[e, s - 1].reshape(T, Fk).astype(F32)
            total = total.astype(BF16)
            pieces += [total[:, g * L:(g + 1) * L] for g in range(G)]
        stacked = jnp.concatenate(pieces, axis=0)
        xsend[c] = jnp.dot(
            perm_send[...], stacked, preferred_element_type=F32
        ).astype(BF16)
        mine = pl.ds(pl.multiple_of(ex * R, R), R)

        def send(s, carry):
            to = lax.rem(ex + s, n_ex)
            theirs = pl.ds(pl.multiple_of(to * R, R), R)
            pltpu.make_async_remote_copy(
                src_ref=xsend.at[c, theirs], dst_ref=xrecv.at[c, mine],
                send_sem=xs_sem.at[c], recv_sem=xr_sem.at[c],
                device_id=(to, dp), device_id_type=MESH,
            ).start()
            return carry

        lax.fori_loop(1, n_ex, send, 0, unroll=n_ex <= 16)
        xrecv[c, mine] = xsend[c, mine]

    total = None
    for c in range(chunks):
        most = xrecv.at[c, pl.ds(0, (n_ex - 1) * R)]
        pltpu.make_async_copy(most, most, xr_sem.at[c]).wait()
        term = jnp.dot(perm_recv[c], xrecv[c], preferred_element_type=F32)
        total = term if total is None else total + term
    total = total.astype(BF16)
    per_token = jnp.concatenate(
        [total[g * Tk * E:(g + 1) * Tk * E] for g in range(G)], axis=1
    )
    full = lax.dot_general(per_token, per_token, nt, preferred_element_type=F32)
    lane = lax.broadcasted_iota(jnp.int32, (E, Tk * E), 1)
    row = lax.broadcasted_iota(jnp.int32, (E, Tk * E), 0)
    gram = jnp.zeros((E, Tk * E), F32)
    for j in range(Tk):
        gram = jnp.where((lane >> lE) == j, full[j * E:(j + 1) * E], gram)
    gsend[...] = gram
    g_copies = []
    for s in range(1, n_dp):
        copy = pltpu.make_async_remote_copy(
            src_ref=gsend, dst_ref=grecv.at[s - 1],
            send_sem=gs_sem.at[s - 1], recv_sem=gr_sem.at[s - 1],
            device_id=(ex, dp_peer(s)), device_id_type=MESH,
        )
        copy.start()
        g_copies.append(copy)
    for copy in tok_copies:
        copy.wait_send()
    for copy in y_copies.values():
        copy.wait_send()
    for c in range(chunks):
        most = xsend.at[c, pl.ds(0, (n_ex - 1) * R)]
        pltpu.make_async_copy(most, most, xs_sem.at[c]).wait()
    for s in range(1, n_dp):
        g_copies[s - 1].wait_recv()
        gram += grecv[s - 1]
    diagonal = jnp.where((lane & (E - 1)) == row, gram, 0.0)
    along = lax.rsqrt(jnp.sum(diagonal, axis=0, keepdims=True) + 1e-06)
    for j in range(Tk):
        block = slice(j * E, (j + 1) * E)
        down = lax.rsqrt(jnp.sum(diagonal[:, block], axis=1, keepdims=True) + 1e-06)
        out_ref[j] = gram[:, block] * down * along[:, block]
    for copy in g_copies:
        copy.wait_send()


def shards(n_dp, n_ex, tokens, w_gate, w_up, w_down):
    Tl, D = tokens.shape
    E_loc, H, _ = w_gate.shape
    T = Tl * n_dp
    Tk = T // n_ex
    Fk = D // n_dp
    ec = 1 if Tk * (Fk // 128) >= 16 else E_loc
    G = max(1, 16 // (Tk * ec))
    L = Fk // G
    R = ec * G * Tk
    E = n_ex * E_loc
    chunks = E_loc // ec
    cfg = (n_dp, n_ex, T, Tl, D, H, E_loc, ec, G, L, Tk)
    dma = pltpu.SemaphoreType.DMA
    peers = n_dp - 1
    return pl.pallas_call(
        functools.partial(kernel, cfg),
        out_shape=jax.ShapeDtypeStruct((Tk, E, E), F32),
        in_specs=[pl.BlockSpec(memory_space=pl.ANY)] * 4,
        out_specs=pl.BlockSpec(memory_space=pltpu.VMEM),
        scratch_shapes=[
            pltpu.VMEM((n_dp, Tl, D), BF16),
            pltpu.VMEM((E_loc, H, D), BF16),
            pltpu.VMEM((E_loc, H, D), BF16),
            pltpu.VMEM((E_loc, H, D), BF16),
            pltpu.VMEM((ec * G * T, ec * G * T), BF16),
            pltpu.VMEM((chunks, G * Tk * E, n_ex * R), BF16),
            pltpu.VMEM((E_loc, n_dp, Tl, Fk), F32),
            pltpu.VMEM((E_loc, peers, n_dp, Tl, Fk), BF16),
            pltpu.VMEM((E_loc, peers, n_dp, Tl, Fk), BF16),
            pltpu.VMEM((chunks, n_ex * R, L), BF16),
            pltpu.VMEM((chunks, n_ex * R, L), BF16),
            pltpu.VMEM((E, Tk * E), F32),
            pltpu.VMEM((peers, E, Tk * E), F32),
            dma((E_loc, 3)),
            dma,
            dma((peers,)),
            dma((peers,)),
            dma((E_loc, peers, n_dp)),
            dma((E_loc, peers, n_dp)),
            dma((chunks,)),
            dma((chunks,)),
            dma((peers,)),
            dma((peers,)),
        ],
        compiler_params=pltpu.CompilerParams(
            collective_id=0, has_side_effects=True, vmem_limit_bytes=60 * 1024 * 1024
        ),
        cost_estimate=pl.CostEstimate(
            flops=6 * E_loc * T * D * H, bytes_accessed=6 * E_loc * H * D,
            transcendentals=E_loc * T * H,
        ),
    )(tokens, w_gate, w_up, w_down)


def solution(mesh):
    placed = (
        P("dp", None),
        P("expert", "dp", None),
        P("expert", "dp", None),
        P("expert", "dp", None),
    )
    return jax.shard_map(
        functools.partial(shards, mesh.shape["dp"], mesh.shape["expert"]),
        mesh=mesh, in_specs=placed, out_specs=P("expert", None, None), check_vma=False,
    )
```

```python
import functools

import jax
import jax.numpy as jnp
from jax import lax
from jax.experimental import pallas as pl
from jax.experimental.pallas import tpu as pltpu
from jax.sharding import PartitionSpec as P

F32 = jnp.float32
BF16 = jnp.bfloat16
MESH = pl.DeviceIdType.MESH


def log2(n):
    assert n & (n - 1) == 0
    return n.bit_length() - 1


def matrix_of(rows, cols, want, keep=None):
    r = lax.broadcasted_iota(jnp.int32, (rows, cols), 0)
    q = lax.broadcasted_iota(jnp.int32, (rows, cols), 1)
    hit = q == want(r)
    if keep is not None:
        hit = hit & keep(r)
    return jnp.where(hit, 1.0, 0.0).astype(BF16)


def kernel(cfg, tok_hbm, wg_hbm, wu_hbm, wd_hbm, out_ref,
           tok, wg, wu, wd, perm_send, perm_recv, own, ysend, yrecv, xsend, xrecv,
           gsend, grecv,
           w_sem, t_sem, ts_sem, tr_sem, ys_sem, yr_sem, xs_sem, xr_sem, gs_sem, gr_sem):
    n_dp, n_ex, T, Tl, D, H, E_loc, ec, G, L, Tk = cfg
    E = n_ex * E_loc
    Fk = D // n_dp
    R = ec * G * Tk
    chunks = E_loc // ec
    dp = lax.axis_index("dp")
    ex = lax.axis_index("expert")

    def dp_peer(s):
        return lax.rem(dp + s, n_dp)

    barrier = pltpu.get_barrier_semaphore()
    for s in range(1, n_dp):
        pl.semaphore_signal(barrier, inc=1, device_id=(ex, dp_peer(s)), device_id_type=MESH)

    def greet(s, carry):
        pl.semaphore_signal(
            barrier, inc=1, device_id=(lax.rem(ex + s, n_ex), dp), device_id_type=MESH
        )
        return carry

    lax.fori_loop(1, n_ex, greet, 0)

    own_tok = pltpu.make_async_copy(tok_hbm, tok.at[0], t_sem)
    own_tok.start()
    loads = {}
    for e in range(E_loc):
        for k, (src, dst) in enumerate(((wg_hbm, wg), (wu_hbm, wu), (wd_hbm, wd))):
            loads[e, k] = pltpu.make_async_copy(src.at[e], dst.at[e], w_sem.at[e, k])
            loads[e, k].start()

    pl.semaphore_wait(barrier, n_dp - 1 + n_ex - 1)

    tok_copies = []
    for s in range(1, n_dp):
        copy = pltpu.make_async_remote_copy(
            src_ref=tok_hbm, dst_ref=tok.at[s],
            send_sem=ts_sem.at[s - 1], recv_sem=tr_sem.at[s - 1],
            device_id=(ex, dp_peer(s)), device_id_type=MESH,
        )
        copy.start()
        tok_copies.append(copy)

    nt = (((1,), (1,)), ((), ()))
    y_copies = {}

    def hidden_of(tokens, e):
        gate = lax.dot_general(tokens, wg[e], nt, preferred_element_type=F32)
        up = lax.dot_general(tokens, wu[e], nt, preferred_element_type=F32)
        return (gate / (1.0 + jnp.exp(-gate)) * up).astype(BF16)

    def project_theirs(hidden, e, slots):
        for s in range(1, n_dp):
            cols = pl.ds(pl.multiple_of(dp_peer(s) * Fk, Fk), Fk)
            part = jnp.dot(hidden, wd[e, :, cols], preferred_element_type=F32).astype(BF16)
            for n, k in enumerate(slots):
                owner = lax.rem(dp + n_dp - k, n_dp)
                ysend[e, s - 1, owner] = part[n * Tl:(n + 1) * Tl]
                copy = pltpu.make_async_remote_copy(
                    src_ref=ysend.at[e, s - 1, owner], dst_ref=yrecv.at[e, s - 1, owner],
                    send_sem=ys_sem.at[e, s - 1, k], recv_sem=yr_sem.at[e, s - 1, k],
                    device_id=(ex, dp_peer(s)), device_id_type=MESH,
                )
                copy.start()
                y_copies[e, s, k] = copy

    def project_mine(hidden, e, slots):
        cols = pl.ds(pl.multiple_of(dp * Fk, Fk), Fk)
        part = jnp.dot(hidden, wd[e, :, cols], preferred_element_type=F32)
        for n, k in enumerate(slots):
            own[e, lax.rem(dp + n_dp - k, n_dp)] = part[n * Tl:(n + 1) * Tl]

    own_tok.wait()
    for e in range(E_loc):
        loads[e, 0].wait()
        loads[e, 1].wait()
        hidden = hidden_of(tok[0], e)
        loads[e, 2].wait()
        project_theirs(hidden, e, (0,))
        project_mine(hidden, e, (0,))

    GE = ec * G
    rows = GE * T
    lR, lTk = log2(R), log2(Tk)
    perm_send[...] = matrix_of(
        rows, rows,
        lambda r: ((r >> lTk) & (GE - 1)) * T + (r >> lR) * Tk + (r & (Tk - 1)),
    )
    for copy in tok_copies:
        copy.wait_recv()
    if n_dp > 1:
        hidden = []
        for e in range(E_loc):
            hidden.append(hidden_of(tok[1:].reshape(T - Tl, D), e))
            project_theirs(hidden[e], e, range(1, n_dp))
        for e in range(E_loc):
            project_mine(hidden[e], e, range(1, n_dp))

    for c in range(chunks):
        pieces = []
        for e in range(c * ec, (c + 1) * ec):
            total = own[e].reshape(T, Fk)
            for s in range(1, n_dp):
                for k in range(n_dp):
                    y_copies[e, s, k].wait_recv()
                total += yrecv[e, s - 1].reshape(T, Fk).astype(F32)
            total = total.astype(BF16)
            pieces += [total[:, g * L:(g + 1) * L] for g in range(G)]
        stacked = jnp.concatenate(pieces, axis=0)
        xsend[c] = jnp.dot(
            perm_send[...], stacked, preferred_element_type=F32
        ).astype(BF16)
        mine = pl.ds(pl.multiple_of(ex * R, R), R)

        def send(s, carry):
            to = lax.rem(ex + s, n_ex)
            theirs = pl.ds(pl.multiple_of(to * R, R), R)
            pltpu.make_async_remote_copy(
                src_ref=xsend.at[c, theirs], dst_ref=xrecv.at[c, mine],
                send_sem=xs_sem.at[c], recv_sem=xr_sem.at[c],
                device_id=(to, dp), device_id_type=MESH,
            ).start()
            return carry

        lax.fori_loop(1, n_ex, send, 0, unroll=n_ex <= 16)
        xrecv[c, mine] = xsend[c, mine]

    lE, lEl, lec = log2(E), log2(E_loc), log2(ec)

    for c in range(chunks):
        def want(r):
            g = r >> (lTk + lE)
            j = (r >> lE) & (Tk - 1)
            e = r & (E - 1)
            el = e & (ec - 1)
            return (e >> lEl) * R + (el * G + g) * Tk + j

        perm_recv[c] = matrix_of(
            G * Tk * E, n_ex * R, want,
            lambda r: ((r & (E_loc - 1)) >> lec) == c,
        )

    total = None
    for c in range(chunks):
        most = xrecv.at[c, pl.ds(0, (n_ex - 1) * R)]
        pltpu.make_async_copy(most, most, xr_sem.at[c]).wait()
        term = jnp.dot(perm_recv[c], xrecv[c], preferred_element_type=F32)
        total = term if total is None else total + term
    total = total.astype(BF16)
    per_token = jnp.concatenate(
        [total[g * Tk * E:(g + 1) * Tk * E] for g in range(G)], axis=1
    )
    full = lax.dot_general(per_token, per_token, nt, preferred_element_type=F32)
    lane = lax.broadcasted_iota(jnp.int32, (E, Tk * E), 1)
    row = lax.broadcasted_iota(jnp.int32, (E, Tk * E), 0)
    gram = jnp.zeros((E, Tk * E), F32)
    for j in range(Tk):
        gram = jnp.where((lane >> lE) == j, full[j * E:(j + 1) * E], gram)
    gsend[...] = gram
    g_copies = []
    for s in range(1, n_dp):
        copy = pltpu.make_async_remote_copy(
            src_ref=gsend, dst_ref=grecv.at[s - 1],
            send_sem=gs_sem.at[s - 1], recv_sem=gr_sem.at[s - 1],
            device_id=(ex, dp_peer(s)), device_id_type=MESH,
        )
        copy.start()
        g_copies.append(copy)
    for copy in tok_copies:
        copy.wait_send()
    for copy in y_copies.values():
        copy.wait_send()
    for c in range(chunks):
        most = xsend.at[c, pl.ds(0, (n_ex - 1) * R)]
        pltpu.make_async_copy(most, most, xs_sem.at[c]).wait()
    for s in range(1, n_dp):
        g_copies[s - 1].wait_recv()
        gram += grecv[s - 1]
    diagonal = jnp.where((lane & (E - 1)) == row, gram, 0.0)
    along = lax.rsqrt(jnp.sum(diagonal, axis=0, keepdims=True) + 1e-06)
    for j in range(Tk):
        block = slice(j * E, (j + 1) * E)
        down = lax.rsqrt(jnp.sum(diagonal[:, block], axis=1, keepdims=True) + 1e-06)
        out_ref[j] = gram[:, block] * down * along[:, block]
    for copy in g_copies:
        copy.wait_send()


def shards(n_dp, n_ex, tokens, w_gate, w_up, w_down):
    Tl, D = tokens.shape
    E_loc, H, _ = w_gate.shape
    T = Tl * n_dp
    Tk = T // n_ex
    Fk = D // n_dp
    ec = E_loc
    G = max(1, 16 // (Tk * ec))
    L = Fk // G
    R = ec * G * Tk
    E = n_ex * E_loc
    chunks = E_loc // ec
    cfg = (n_dp, n_ex, T, Tl, D, H, E_loc, ec, G, L, Tk)
    dma = pltpu.SemaphoreType.DMA
    peers = n_dp - 1
    return pl.pallas_call(
        functools.partial(kernel, cfg),
        out_shape=jax.ShapeDtypeStruct((Tk, E, E), F32),
        in_specs=[pl.BlockSpec(memory_space=pl.ANY)] * 4,
        out_specs=pl.BlockSpec(memory_space=pltpu.VMEM),
        scratch_shapes=[
            pltpu.VMEM((n_dp, Tl, D), BF16),
            pltpu.VMEM((E_loc, H, D), BF16),
            pltpu.VMEM((E_loc, H, D), BF16),
            pltpu.VMEM((E_loc, H, D), BF16),
            pltpu.VMEM((ec * G * T, ec * G * T), BF16),
            pltpu.VMEM((chunks, G * Tk * E, n_ex * R), BF16),
            pltpu.VMEM((E_loc, n_dp, Tl, Fk), F32),
            pltpu.VMEM((E_loc, peers, n_dp, Tl, Fk), BF16),
            pltpu.VMEM((E_loc, peers, n_dp, Tl, Fk), BF16),
            pltpu.VMEM((chunks, n_ex * R, L), BF16),
            pltpu.VMEM((chunks, n_ex * R, L), BF16),
            pltpu.VMEM((E, Tk * E), F32),
            pltpu.VMEM((peers, E, Tk * E), F32),
            dma((E_loc, 3)),
            dma,
            dma((peers,)),
            dma((peers,)),
            dma((E_loc, peers, n_dp)),
            dma((E_loc, peers, n_dp)),
            dma((chunks,)),
            dma((chunks,)),
            dma((peers,)),
            dma((peers,)),
        ],
        compiler_params=pltpu.CompilerParams(
            collective_id=0, has_side_effects=True, vmem_limit_bytes=60 * 1024 * 1024
        ),
        cost_estimate=pl.CostEstimate(
            flops=6 * E_loc * T * D * H, bytes_accessed=6 * E_loc * H * D,
            transcendentals=E_loc * T * H,
        ),
    )(tokens, w_gate, w_up, w_down)


def solution(mesh):
    placed = (
        P("dp", None),
        P("expert", "dp", None),
        P("expert", "dp", None),
        P("expert", "dp", None),
    )
    return jax.shard_map(
        functools.partial(shards, mesh.shape["dp"], mesh.shape["expert"]),
        mesh=mesh, in_specs=placed, out_specs=P("expert", None, None), check_vma=False,
    )
```

```python
import functools

import jax
import jax.numpy as jnp
from jax import lax
from jax.experimental import pallas as pl
from jax.experimental.pallas import tpu as pltpu
from jax.sharding import PartitionSpec as P

F32 = jnp.float32
BF16 = jnp.bfloat16
MESH = pl.DeviceIdType.MESH


def log2(n):
    assert n & (n - 1) == 0
    return n.bit_length() - 1


def matrix_of(rows, cols, want, keep=None):
    r = lax.broadcasted_iota(jnp.int32, (rows, cols), 0)
    q = lax.broadcasted_iota(jnp.int32, (rows, cols), 1)
    hit = q == want(r)
    if keep is not None:
        hit = hit & keep(r)
    return jnp.where(hit, 1.0, 0.0).astype(BF16)


def kernel(cfg, tok_hbm, wg_hbm, wu_hbm, wd_hbm, out_ref,
           tok, wg, wu, wd, perm_send, perm_recv, own, ysend, yrecv, xsend, xrecv,
           gsend, grecv,
           w_sem, t_sem, ts_sem, tr_sem, ys_sem, yr_sem, xs_sem, xr_sem, gs_sem, gr_sem):
    n_dp, n_ex, T, Tl, D, H, E_loc, ec, G, L, Tk = cfg
    E = n_ex * E_loc
    Fk = D // n_dp
    R = ec * G * Tk
    chunks = E_loc // ec
    dp = lax.axis_index("dp")
    ex = lax.axis_index("expert")

    def dp_peer(s):
        return lax.rem(dp + s, n_dp)

    barrier = pltpu.get_barrier_semaphore()
    for s in range(1, n_dp):
        pl.semaphore_signal(barrier, inc=1, device_id=(ex, dp_peer(s)), device_id_type=MESH)

    def greet(s, carry):
        pl.semaphore_signal(
            barrier, inc=1, device_id=(lax.rem(ex + s, n_ex), dp), device_id_type=MESH
        )
        return carry

    lax.fori_loop(1, n_ex, greet, 0)

    own_tok = pltpu.make_async_copy(tok_hbm, tok.at[0], t_sem)
    own_tok.start()
    loads = {}
    for e in range(E_loc):
        for k, (src, dst) in enumerate(((wg_hbm, wg), (wu_hbm, wu), (wd_hbm, wd))):
            loads[e, k] = pltpu.make_async_copy(src.at[e], dst.at[e], w_sem.at[e, k])
            loads[e, k].start()

    pl.semaphore_wait(barrier, n_dp - 1 + n_ex - 1)

    tok_copies = []
    for s in range(1, n_dp):
        copy = pltpu.make_async_remote_copy(
            src_ref=tok_hbm, dst_ref=tok.at[s],
            send_sem=ts_sem.at[s - 1], recv_sem=tr_sem.at[s - 1],
            device_id=(ex, dp_peer(s)), device_id_type=MESH,
        )
        copy.start()
        tok_copies.append(copy)

    nt = (((1,), (1,)), ((), ()))
    y_copies = {}

    def hidden_of(tokens, e):
        gate = lax.dot_general(tokens, wg[e], nt, preferred_element_type=F32)
        up = lax.dot_general(tokens, wu[e], nt, preferred_element_type=F32)
        return (gate / (1.0 + jnp.exp(-gate)) * up).astype(BF16)

    def project_theirs(hidden, e, slots):
        for s in range(1, n_dp):
            cols = pl.ds(pl.multiple_of(dp_peer(s) * Fk, Fk), Fk)
            part = jnp.dot(hidden, wd[e, :, cols], preferred_element_type=F32).astype(BF16)
            for n, k in enumerate(slots):
                owner = lax.rem(dp + n_dp - k, n_dp)
                ysend[e, s - 1, owner] = part[n * Tl:(n + 1) * Tl]
                copy = pltpu.make_async_remote_copy(
                    src_ref=ysend.at[e, s - 1, owner], dst_ref=yrecv.at[e, s - 1, owner],
                    send_sem=ys_sem.at[e, s - 1, k], recv_sem=yr_sem.at[e, s - 1, k],
                    device_id=(ex, dp_peer(s)), device_id_type=MESH,
                )
                copy.start()
                y_copies[e, s, k] = copy

    def project_mine(hidden, e, slots):
        cols = pl.ds(pl.multiple_of(dp * Fk, Fk), Fk)
        part = jnp.dot(hidden, wd[e, :, cols], preferred_element_type=F32)
        for n, k in enumerate(slots):
            own[e, lax.rem(dp + n_dp - k, n_dp)] = part[n * Tl:(n + 1) * Tl]

    own_tok.wait()
    first = []
    for e in range(E_loc):
        loads[e, 0].wait()
        loads[e, 1].wait()
        hidden = hidden_of(tok[0], e)
        loads[e, 2].wait()
        project_theirs(hidden, e, (0,))
        first.append(hidden)

    GE = ec * G
    rows = GE * T
    lR, lTk = log2(R), log2(Tk)
    perm_send[...] = matrix_of(
        rows, rows,
        lambda r: ((r >> lTk) & (GE - 1)) * T + (r >> lR) * Tk + (r & (Tk - 1)),
    )
    for copy in tok_copies:
        copy.wait_recv()
    both = []
    for e in range(E_loc):
        both.append(first[e])
        if n_dp > 1:
            rest = hidden_of(tok[1:].reshape(T - Tl, D), e)
            project_theirs(rest, e, range(1, n_dp))
            both[e] = jnp.concatenate([first[e], rest], axis=0)
    for e in range(E_loc):
        project_mine(both[e], e, range(n_dp))

    for c in range(chunks):
        pieces = []
        for e in range(c * ec, (c + 1) * ec):
            total = own[e].reshape(T, Fk)
            for s in range(1, n_dp):
                for k in range(n_dp):
                    y_copies[e, s, k].wait_recv()
                total += yrecv[e, s - 1].reshape(T, Fk).astype(F32)
            total = total.astype(BF16)
            pieces += [total[:, g * L:(g + 1) * L] for g in range(G)]
        stacked = jnp.concatenate(pieces, axis=0)
        xsend[c] = jnp.dot(
            perm_send[...], stacked, preferred_element_type=F32
        ).astype(BF16)
        mine = pl.ds(pl.multiple_of(ex * R, R), R)

        def send(s, carry):
            to = lax.rem(ex + s, n_ex)
            theirs = pl.ds(pl.multiple_of(to * R, R), R)
            pltpu.make_async_remote_copy(
                src_ref=xsend.at[c, theirs], dst_ref=xrecv.at[c, mine],
                send_sem=xs_sem.at[c], recv_sem=xr_sem.at[c],
                device_id=(to, dp), device_id_type=MESH,
            ).start()
            return carry

        lax.fori_loop(1, n_ex, send, 0, unroll=n_ex <= 16)
        xrecv[c, mine] = xsend[c, mine]

    lE, lEl, lec = log2(E), log2(E_loc), log2(ec)

    for c in range(chunks):
        def want(r):
            g = r >> (lTk + lE)
            j = (r >> lE) & (Tk - 1)
            e = r & (E - 1)
            el = e & (ec - 1)
            return (e >> lEl) * R + (el * G + g) * Tk + j

        perm_recv[c] = matrix_of(
            G * Tk * E, n_ex * R, want,
            lambda r: ((r & (E_loc - 1)) >> lec) == c,
        )

    total = None
    for c in range(chunks):
        most = xrecv.at[c, pl.ds(0, (n_ex - 1) * R)]
        pltpu.make_async_copy(most, most, xr_sem.at[c]).wait()
        term = jnp.dot(perm_recv[c], xrecv[c], preferred_element_type=F32)
        total = term if total is None else total + term
    total = total.astype(BF16)
    per_token = jnp.concatenate(
        [total[g * Tk * E:(g + 1) * Tk * E] for g in range(G)], axis=1
    )
    full = lax.dot_general(per_token, per_token, nt, preferred_element_type=F32)
    lane = lax.broadcasted_iota(jnp.int32, (E, Tk * E), 1)
    row = lax.broadcasted_iota(jnp.int32, (E, Tk * E), 0)
    gram = jnp.zeros((E, Tk * E), F32)
    for j in range(Tk):
        gram = jnp.where((lane >> lE) == j, full[j * E:(j + 1) * E], gram)
    gsend[...] = gram
    g_copies = []
    for s in range(1, n_dp):
        copy = pltpu.make_async_remote_copy(
            src_ref=gsend, dst_ref=grecv.at[s - 1],
            send_sem=gs_sem.at[s - 1], recv_sem=gr_sem.at[s - 1],
            device_id=(ex, dp_peer(s)), device_id_type=MESH,
        )
        copy.start()
        g_copies.append(copy)
    for copy in tok_copies:
        copy.wait_send()
    for copy in y_copies.values():
        copy.wait_send()
    for c in range(chunks):
        most = xsend.at[c, pl.ds(0, (n_ex - 1) * R)]
        pltpu.make_async_copy(most, most, xs_sem.at[c]).wait()
    for s in range(1, n_dp):
        g_copies[s - 1].wait_recv()
        gram += grecv[s - 1]
    diagonal = jnp.where((lane & (E - 1)) == row, gram, 0.0)
    along = lax.rsqrt(jnp.sum(diagonal, axis=0, keepdims=True) + 1e-06)
    for j in range(Tk):
        block = slice(j * E, (j + 1) * E)
        down = lax.rsqrt(jnp.sum(diagonal[:, block], axis=1, keepdims=True) + 1e-06)
        out_ref[j] = gram[:, block] * down * along[:, block]
    for copy in g_copies:
        copy.wait_send()


def shards(n_dp, n_ex, tokens, w_gate, w_up, w_down):
    Tl, D = tokens.shape
    E_loc, H, _ = w_gate.shape
    T = Tl * n_dp
    Tk = T // n_ex
    Fk = D // n_dp
    ec = E_loc
    G = max(1, 16 // (Tk * ec))
    L = Fk // G
    R = ec * G * Tk
    E = n_ex * E_loc
    chunks = E_loc // ec
    cfg = (n_dp, n_ex, T, Tl, D, H, E_loc, ec, G, L, Tk)
    dma = pltpu.SemaphoreType.DMA
    peers = n_dp - 1
    return pl.pallas_call(
        functools.partial(kernel, cfg),
        out_shape=jax.ShapeDtypeStruct((Tk, E, E), F32),
        in_specs=[pl.BlockSpec(memory_space=pl.ANY)] * 4,
        out_specs=pl.BlockSpec(memory_space=pltpu.VMEM),
        scratch_shapes=[
            pltpu.VMEM((n_dp, Tl, D), BF16),
            pltpu.VMEM((E_loc, H, D), BF16),
            pltpu.VMEM((E_loc, H, D), BF16),
            pltpu.VMEM((E_loc, H, D), BF16),
            pltpu.VMEM((ec * G * T, ec * G * T), BF16),
            pltpu.VMEM((chunks, G * Tk * E, n_ex * R), BF16),
            pltpu.VMEM((E_loc, n_dp, Tl, Fk), F32),
            pltpu.VMEM((E_loc, peers, n_dp, Tl, Fk), BF16),
            pltpu.VMEM((E_loc, peers, n_dp, Tl, Fk), BF16),
            pltpu.VMEM((chunks, n_ex * R, L), BF16),
            pltpu.VMEM((chunks, n_ex * R, L), BF16),
            pltpu.VMEM((E, Tk * E), F32),
            pltpu.VMEM((peers, E, Tk * E), F32),
            dma((E_loc, 3)),
            dma,
            dma((peers,)),
            dma((peers,)),
            dma((E_loc, peers, n_dp)),
            dma((E_loc, peers, n_dp)),
            dma((chunks,)),
            dma((chunks,)),
            dma((peers,)),
            dma((peers,)),
        ],
        compiler_params=pltpu.CompilerParams(
            collective_id=0, has_side_effects=True, vmem_limit_bytes=60 * 1024 * 1024
        ),
        cost_estimate=pl.CostEstimate(
            flops=6 * E_loc * T * D * H, bytes_accessed=6 * E_loc * H * D,
            transcendentals=E_loc * T * H,
        ),
    )(tokens, w_gate, w_up, w_down)


def solution(mesh):
    placed = (
        P("dp", None),
        P("expert", "dp", None),
        P("expert", "dp", None),
        P("expert", "dp", None),
    )
    return jax.shard_map(
        functools.partial(shards, mesh.shape["dp"], mesh.shape["expert"]),
        mesh=mesh, in_specs=placed, out_specs=P("expert", None, None), check_vma=False,
    )
```
